32 devices in a mesh: row: 2 (over x), col: 16 (over z, y, core).
Axes of the slice: x: 2, y: 2, z: 4, core: 2. Of those that a mesh axis runs over, the one named last changes fastest.
Arguments:
- pair: float32 [128, 128, 128], P('row', 'col'), may hold values from -6 to 6
- single: float32 [128, 384], P(('row', 'col')), may hold values from -6 to 6
- target_bins: int32 [128, 128], P('row', 'col'), may hold values from 0 to 63
- token_pad: int32 [128], P(('row', 'col')), may hold values from 0 to 1, as said below
- w_gate: float32 [128, 512], replicated, may hold values from -0.5 to 0.5
- w_up: float32 [128, 512], replicated, may hold values from -0.5 to 0.5
- w_out: float32 [512, 128], replicated, may hold values from -0.25 to 0.25
- w_bias: float32 [128, 16], replicated, may hold values from -25 to 25
- w_query: float32 [384, 384], replicated, may hold values from -0.3125 to 0.3125
- w_key: float32 [384, 384], replicated, may hold values from -0.3125 to 0.3125
- w_value: float32 [384, 384], replicated, may hold values from -0.3125 to 0.3125
- w_gating: float32 [384, 384], replicated, may hold values from -0.3125 to 0.3125
- w_attn_out: float32 [384, 384], replicated, may hold values from -0.3125 to 0.3125
- w_dist: float32 [128, 64], replicated, may hold values from -12 to 12
- b_dist: float32 [64], replicated, may hold values from -2 to 2
Outputs:
- pair_out: float32 [128, 128, 128], P('row', 'col')
- single_out: float32 [128, 384], P(('row', 'col'))
The draws below stay inside these ranges and needn't reach their ends.
Inputs may be any that keep to these rules, and one draw needn't show every extreme that they name: `token_pad`: 1 for the first tokens and 0 for the rest, with at least 64 ones.
All inputs are finite; a program needn't handle non-finite values.
Results may differ from the reference program's by a relative error of at most 0.0003.
Values sent between devices are 32-bit elements; how exact they have to be, the bound alone decides.
A program may use at most 64 MiB of HBM per device.

```python
from functools import partial
import jax
import jax.numpy as jnp
from jax import lax

PAIR = 128
TRANS = 512
SINGLE = 384
HEADS = 16
HEAD_DIM = 24
BINS = 64
TOK_DEV = 4
N = 128
N_COL = 16


def draw_token_pad(key, part):
    length = jax.random.randint(jax.random.fold_in(key, 11), (), N // 2, N + 1)
    return (jnp.arange(N, dtype=jnp.int32) < length).astype(jnp.int32)


def draw_w_bias(key, part):
    base = jnp.clip(jax.random.normal(jax.random.fold_in(key, 23), (PAIR, HEADS), jnp.float32), -4.0, 4.0) * PAIR ** (-0.5)
    return base


def draw_w_dist(key, part):
    base = jnp.clip(jax.random.normal(jax.random.fold_in(key, 31), (PAIR, BINS), jnp.float32), -4.0, 4.0) * 0.25
    return base


def touch_ends(values, stream_key, low, largest):
    index_at = [jax.random.randint(jax.random.fold_in(stream_key, axis), (), 0, length) for axis, length in enumerate(values.shape)]
    longest = values.shape.index(max(values.shape))
    next_to = index_at[:longest] + [(index_at[longest] + 1) % values.shape[longest]] + index_at[longest + 1:]
    return values.at[tuple(index_at)].set(low).at[tuple(next_to)].set(largest)


def block_scale(rng, extent, shards, least, high):
    def one(dim, parts):
        steps = jax.random.uniform(jax.random.fold_in(jax.random.fold_in(rng, 6), dim), (parts,), jnp.float32, least / len(shards), high / len(shards))
        return jnp.repeat(jnp.exp(steps), extent[dim] // parts).reshape((-1,) + (1,) * (len(extent) - dim - 1))

    gain = one(*shards[0])
    for cut in shards[1:]:
        gain = gain * one(*cut)
    return gain


def scatter_about(stream_key, shape, spread, bound, pieces=(), held_as=jnp.bfloat16):
    loudness = block_scale(stream_key, shape, pieces, -0.22, 0.18) if pieces else 1.0
    values = jax.random.normal(stream_key, shape, jnp.float32) * spread * loudness
    return jnp.minimum(jnp.maximum(values, -bound), bound).astype(held_as)


def setup_inputs(seed: int = 0) -> dict:
    seeds = jax.random.split(jax.random.key(seed), 16)
    return {
        "pair": scatter_about(seeds[0], (N, N, PAIR), 1.0, 6.0, ((0, 2), (1, 16)), jnp.float32),
        "single": scatter_about(seeds[1], (N, SINGLE), 1.0, 6.0, ((0, 32),), jnp.float32),
        "target_bins": touch_ends(jax.random.randint(seeds[2], (N, N), 0, BINS), jax.random.fold_in(seeds[2], 1), 0, BINS - 1).astype(jnp.int32),
        "token_pad": draw_token_pad(jax.random.fold_in(seeds[15], 71), 0),
        "w_gate": scatter_about(seeds[4], (PAIR, TRANS), PAIR ** -0.5, 0.5, (), jnp.float32),
        "w_up": scatter_about(seeds[5], (PAIR, TRANS), PAIR ** -0.5, 0.5, (), jnp.float32),
        "w_out": scatter_about(seeds[6], (TRANS, PAIR), TRANS ** -0.5, 0.25, (), jnp.float32),
        "w_bias": draw_w_bias(jax.random.fold_in(seeds[15], 71), 0),
        "w_query": scatter_about(seeds[8], (SINGLE, SINGLE), SINGLE ** -0.5, 0.3125, (), jnp.float32),
        "w_key": scatter_about(seeds[9], (SINGLE, SINGLE), SINGLE ** -0.5, 0.3125, (), jnp.float32),
        "w_value": scatter_about(seeds[10], (SINGLE, SINGLE), SINGLE ** -0.5, 0.3125, (), jnp.float32),
        "w_gating": scatter_about(seeds[11], (SINGLE, SINGLE), SINGLE ** -0.5, 0.3125, (), jnp.float32),
        "w_attn_out": scatter_about(seeds[12], (SINGLE, SINGLE), SINGLE ** -0.5, 0.3125, (), jnp.float32),
        "w_dist": draw_w_dist(jax.random.fold_in(seeds[15], 71), 0),
        "b_dist": jnp.clip(jax.random.uniform(seeds[14], (BINS,), jnp.float32, -2.0, 2.0), -2.0, 2.0),
    }


HI = lax.Precision.HIGHEST

def layer_norm(x):
    mean = lax.optimization_barrier(jnp.mean(x, axis=-1, keepdims=True))
    centred = x - mean
    var = lax.optimization_barrier(jnp.mean(centred * centred, axis=-1, keepdims=True))
    return centred * lax.rsqrt(var + 1e-05)

def dense(x, w):
    flat = x.reshape(-1, x.shape[-1])
    out = jnp.dot(flat, w, precision=HI, preferred_element_type=jnp.float32)
    return out.reshape(x.shape[:-1] + (w.shape[1],))

def transition_rows(block, w_gate, w_up, w_out, w_bias):
    normed = layer_norm(block)
    hidden = jax.nn.silu(dense(normed, w_gate)) * dense(normed, w_up)
    mid = block + dense(hidden, w_out)
    bias = dense(layer_norm(mid), w_bias)
    return (mid, bias)

def dist_rows(start, mid, target_bins, pad_float, w_dist, b_dist, block):
    mid_rows = lax.dynamic_slice_in_dim(mid, start, block, 0)
    mid_cols = lax.dynamic_slice_in_dim(mid, start, block, 1)
    proj_rows = dense(mid_rows, w_dist)
    proj_cols = jnp.transpose(dense(mid_cols, w_dist), (1, 0, 2))
    logits = proj_rows + proj_cols + b_dist
    shifted = logits - lax.optimization_barrier(jnp.max(logits, axis=-1, keepdims=True))
    expo = jnp.exp(shifted)
    probs = expo / lax.optimization_barrier(jnp.sum(expo, axis=-1, keepdims=True))
    pad_rows = lax.dynamic_slice_in_dim(pad_float, start, block, 0)
    mask = pad_rows[:, None] * pad_float[None, :]
    bin_ids = jnp.arange(w_dist.shape[1], dtype=jnp.int32)
    t_rows = lax.dynamic_slice_in_dim(target_bins, start, block, 0)
    t_cols = jnp.transpose(lax.dynamic_slice_in_dim(target_bins, start, block, 1))
    onehot = (t_rows[:, :, None] == bin_ids).astype(jnp.float32)
    onehot_flip = (t_cols[:, :, None] == bin_ids).astype(jnp.float32)
    delta = mask[:, :, None] * (2.0 * probs - onehot - onehot_flip)
    return mid_rows + dense(delta, jnp.transpose(w_dist))

def reference(pair, single, target_bins, token_pad, w_gate, w_up, w_out, w_bias, w_query, w_key, w_value, w_gating, w_attn_out, w_dist, b_dist):
    block = TOK_DEV * N_COL // 4
    count = N // block
    blocks = pair.reshape(count, block, N, PAIR)
    mid, bias = lax.map(partial(transition_rows, w_gate=w_gate, w_up=w_up, w_out=w_out, w_bias=w_bias), blocks)
    mid = mid.reshape(N, N, PAIR)
    bias = bias.reshape(N, N, HEADS)
    single_norm = layer_norm(single)
    query = dense(single_norm, w_query).reshape(N, HEADS, HEAD_DIM)
    key = dense(single_norm, w_key).reshape(N, HEADS, HEAD_DIM)
    value = dense(single_norm, w_value).reshape(N, HEADS, HEAD_DIM)
    gating = jax.nn.sigmoid(dense(single_norm, w_gating))
    scores = jnp.einsum('ihd,jhd->ijh', query, key, precision=HI) / jnp.sqrt(jnp.float32(HEAD_DIM)) + bias
    scores = jnp.where((token_pad > 0)[None, :, None], scores, jnp.float32(-1000000000.0))
    top = lax.optimization_barrier(jnp.max(scores, axis=1, keepdims=True))
    expo = jnp.exp(scores - top)
    total = lax.optimization_barrier(jnp.sum(expo, axis=1))
    attended = jnp.einsum('ijh,jhd->ihd', expo, value, precision=HI) / total[:, :, None]
    single_out = single + dense(gating * attended.reshape(N, SINGLE), w_attn_out)
    pad_float = token_pad.astype(jnp.float32)
    starts = (jnp.arange(count) * block).astype(jnp.int32)
    pair_out = lax.map(partial(dist_rows, mid=mid, target_bins=target_bins, pad_float=pad_float, w_dist=w_dist, b_dist=b_dist, block=block), starts)
    pair_out = pair_out.reshape(N, N, PAIR)
    return (pair_out, single_out)
```

```python
import functools

import jax
import jax.numpy as jnp
from jax import lax
from jax.experimental import pallas as pl
from jax.experimental.pallas import tpu as pltpu
from jax.sharding import PartitionSpec as P

MESH = pl.DeviceIdType.MESH
F32 = jnp.float32
BF16 = jnp.bfloat16
NN = (((1,), (0,)), ((), ()))
NT = (((1,), (1,)), ((), ()))
PARTS = 2


def split(x):
    high = x.astype(BF16)
    return high, (x - high.astype(F32)).astype(BF16)


def mm(a, b, dims=NN):
    return lax.dot_general(a, b, dims, preferred_element_type=F32)


def dot3(a, b, dims=NN):
    ah, al = split(a)
    bh, bl = b if isinstance(b, tuple) else split(b)
    return mm(ah, bh, dims) + (mm(al, bh, dims) + mm(ah, bl, dims))


def layer_norm(x):
    mean = jnp.mean(x, axis=-1, keepdims=True)
    centred = x - mean
    var = jnp.mean(centred * centred, axis=-1, keepdims=True)
    return centred * lax.rsqrt(var + 1e-05)


def iota(shape, axis):
    return lax.broadcasted_iota(jnp.int32, shape, axis)


def kernel(n_row, n_col, heads, *refs):
    (pair_h, single_h, target_h, pad_s, gate_h, up_h, wout_h, wbias_h, wq_h, wk_h, wv_h, wg_h, wo_h, wdist_h, bdist_h,
     pair_o, single_o,
     pair_v, single_v, target_v, gate_v, up_v, wout_v, wbias_v, wq_v, wk_v, wv_v, wg_v, wo_v, wdist_v, bdist_v,
     ext, gath, tokens, mid_v, proj_v, flip_v, sbuf, rbuf, bsend, brecv,
     in_sem, g_send, g_recv, b_send, b_recv, p_send, p_recv) = refs
    rows, cols, width = pair_v.shape
    tok, single_width = single_v.shape
    bins = wdist_v.shape[1]
    n_dev = n_row * n_col
    group = rows // cols
    lanes = bsend.shape[2]
    head_dim = single_width // heads
    packed = cols * cols // 2
    r = lax.axis_index("row")
    c = lax.axis_index("col")
    me = r * n_col + c

    sources = (single_h, pair_h, gate_h, up_h, wout_h, target_h, wbias_h, wdist_h, wk_h, wv_h, wq_h, wg_h, wo_h, bdist_h)
    targets = (single_v, pair_v, gate_v, up_v, wout_v, target_v, wbias_v, wdist_v, wk_v, wv_v, wq_v, wg_v, wo_v, bdist_v)
    loads = [pltpu.make_async_copy(a, b, in_sem.at[k]) for k, (a, b) in enumerate(zip(sources, targets))]
    for load in loads:
        load.start()

    barrier = pltpu.get_barrier_semaphore()

    def other(step):
        d = lax.rem(me + step, n_dev)
        return d // n_col, lax.rem(d, n_col)

    def greet(step, carry):
        pl.semaphore_signal(barrier, inc=1, device_id=other(step), device_id_type=MESH)
        return carry

    lax.fori_loop(1, n_dev, greet, 0)

    loads[0].wait()
    row_id = iota((tok, 128), 0)
    pad_tile = jnp.zeros((tok, 128), F32)
    for q in range(tok):
        pad_tile = jnp.where(row_id == q, pad_s[q].astype(F32), pad_tile)
    ext[:, :single_width] = single_v[...]
    ext[:, single_width:] = pad_tile
    gath[me] = ext[...]
    pl.semaphore_wait(barrier, n_dev - 1)

    def share(step, carry):
        pltpu.make_async_remote_copy(ext, gath.at[me], g_send, g_recv, device_id=other(step), device_id_type=MESH).start()
        return carry

    lax.fori_loop(1, n_dev, share, 0)

    for load in loads[1:8]:
        load.wait()

    gate_w = split(gate_v[...])
    up_w = split(up_v[...])
    out_w = split(wout_v[...])
    wdist = wdist_v[...]
    dist_w = split(wdist)
    none = jnp.zeros_like(wdist)
    wide = jnp.concatenate([jnp.concatenate([wdist, none], axis=1), jnp.concatenate([none, wdist], axis=1)], axis=0)
    wide_w = split(wide)
    spread = (iota((heads, lanes), 0) == lax.rem(iota((heads, lanes), 1), heads)).astype(F32)
    bias_rep = lax.dot_general(wbias_v[...], spread, NN, precision=lax.Precision.HIGHEST, preferred_element_type=F32)
    lane_q = iota((width, lanes), 1) // heads
    bias_w = split(jnp.concatenate([jnp.where(lane_q == q, bias_rep, 0.0) for q in range(tok)], axis=0))

    sbuf[:, packed:, :] = jnp.zeros((group, cols, 128), F32)
    sbuf[:, packed:, :cols] = target_v[...].astype(F32).reshape(group, cols, cols)

    part = rows // PARTS
    p_row = c // group
    p_slot = lax.rem(c, group)

    def send_bias(d, carry):
        @pl.when(d != c)
        def _():
            pltpu.make_async_remote_copy(bsend.at[d], brecv.at[c], b_send, b_recv, device_id=(r, d), device_id_type=MESH).start()
        return carry

    def is_self(k):
        return jnp.logical_and(p_row == r, p_slot == k)

    def send_proj(k, carry):
        @pl.when(jnp.logical_not(is_self(k)))
        def _():
            pltpu.make_async_remote_copy(sbuf.at[k], rbuf.at[p_slot], p_send, p_recv, device_id=(p_row, group * r + k), device_id_type=MESH).start()
        return carry

    for s in range(PARTS):
        first = s * part
        x = pair_v[first:first + part].reshape(part * cols, width)
        normed = layer_norm(x)
        g = dot3(normed, gate_w)
        u = dot3(normed, up_w)
        hidden = g / (1.0 + jnp.exp(-g)) * u
        mid = x + dot3(hidden, out_w)
        mid_v[first * cols:(first + part) * cols] = mid
        tiles = part // cols
        halves = mid.reshape(tiles, 2, packed, width)
        both = jnp.concatenate([halves[:, 0].reshape(tiles * packed, width), halves[:, 1].reshape(tiles * packed, width)], axis=1)
        k0 = first // cols
        sbuf[k0:k0 + tiles, :packed, :] = dot3(both, wide_w).reshape(tiles, packed, 2 * bins)
        lax.fori_loop(k0, k0 + tiles, send_proj, 0)
        dests = part // tok
        norm_mid = layer_norm(mid).reshape(dests, tok, cols, width)
        quad = jnp.concatenate([norm_mid[:, q].reshape(dests * cols, width) for q in range(tok)], axis=1)
        d0 = first // tok
        bsend[d0:d0 + dests] = dot3(quad, bias_w).reshape(dests, cols, lanes)
        lax.fori_loop(d0, d0 + dests, send_bias, 0)
        proj_v[first * cols:(first + part) * cols] = dot3(mid, dist_w)

    brecv[c] = bsend[c]

    @pl.when(p_row == r)
    def _():
        rbuf[p_slot] = sbuf[p_slot]

    for load in loads[8:]:
        load.wait()

    def drain(ref, count, sem):
        pltpu.make_async_copy(ref.at[pl.ds(0, count)], ref.at[pl.ds(0, count)], sem).wait()

    drain(gath, n_dev - 1, g_recv)
    step = 8 // tok
    for m in range(n_dev // step):
        tokens[m * 8:(m + 1) * 8, :] = jnp.concatenate([gath[m * step + q] for q in range(step)], axis=0)
    everyone = layer_norm(tokens[:, :single_width])
    key = dot3(everyone, wk_v[...])
    value = dot3(everyone, wv_v[...])
    slots = lanes // heads
    own = jnp.concatenate([single_v[...], jnp.zeros((slots - tok, single_width), F32)], axis=0)
    own_norm = layer_norm(own)
    query = dot3(own_norm, wq_v[...])
    gating = jax.nn.sigmoid(dot3(own_norm, wg_v[...]))
    head_mask = (iota((heads, single_width), 1) // head_dim == iota((heads, single_width), 0)).astype(F32)
    query_wide = (query[:, None, :] * head_mask[None]).reshape(lanes, single_width)
    scores = dot3(key, query_wide, NT) * (1.0 / head_dim ** 0.5)
    pads = tokens[:, single_width:]

    drain(brecv, n_col - 1, b_recv)
    scores = scores + brecv[...].reshape(scores.shape)
    scores = jnp.where(pads > 0.5, scores, -1e9)
    expo = jnp.exp(scores - jnp.max(scores, axis=0, keepdims=True))
    weights = expo / jnp.sum(expo, axis=0, keepdims=True)
    mixed = dot3(jnp.transpose(weights), value).reshape(slots, heads, single_width)
    attended = jnp.sum(mixed * head_mask[None], axis=1)
    single_o[...] = (own + dot3(gating * attended, wo_v[...]))[:tok]

    @pl.when(p_row == r)
    def _():
        drain(rbuf, group - 1, p_recv)

    @pl.when(p_row != r)
    def _():
        drain(rbuf, group, p_recv)

    half = cols // 2
    for q in range(cols):
        piece = rbuf[:, pl.ds(q, half, stride=cols), :]
        flip_v[:, q] = jnp.concatenate([piece[:, :, :bins], piece[:, :, bins:]], axis=1)
    total = rows * cols
    logits = proj_v[...] + flip_v[...].reshape(total, bins) + bdist_v[...]
    expo = jnp.exp(logits - jnp.max(logits, axis=-1, keepdims=True))
    probs = expo / jnp.sum(expo, axis=-1, keepdims=True)
    ones = jnp.ones((cols, bins), BF16)
    lane = iota((rows, cols, cols), 2)
    mine = jnp.broadcast_to(target_v[...].astype(F32)[:, None, :], (rows, cols, cols))
    mine = jnp.where(lane == iota((rows, cols, cols), 1), mine, 0.0).reshape(total, cols)
    mine = mm(mine.astype(BF16), ones)
    theirs = jnp.broadcast_to(rbuf[:, packed:, :cols][:, None], (group, cols, cols, cols))
    fours = (group, cols, cols, cols)
    theirs = jnp.where(iota(fours, 3) == iota(fours, 1), theirs, 0.0).reshape(total, cols)
    theirs = mm(theirs.astype(BF16), ones)
    bin_id = iota((total, bins), 1).astype(F32)
    hot = (mine == bin_id).astype(F32) + (theirs == bin_id).astype(F32)
    pad_i = tokens[pl.ds(pl.multiple_of(r * rows, rows), rows), single_width:single_width + bins]
    pad_j = tokens[pl.ds(pl.multiple_of(c * cols, cols), cols), single_width:single_width + bins]
    mask = (pad_i[:, None, :] * pad_j[None, :, :]).reshape(total, bins)
    delta = mask * (2.0 * probs - hot)
    pair_o[...] = (mid_v[...] + dot3(delta, dist_w, NT)).reshape(rows, cols, width)

    drain(gath, n_dev - 1, g_send)
    drain(brecv, n_col - 1, b_send)

    @pl.when(p_row == r)
    def _():
        drain(rbuf, group - 1, p_send)

    @pl.when(p_row != r)
    def _():
        drain(rbuf, group, p_send)


def per_device(n_row, n_col, pair, single, target_bins, token_pad, *weights):
    rows, cols, width = pair.shape
    tok, single_width = single.shape
    w_gate, w_up, w_out, w_bias, w_query, w_key, w_value, w_gating, w_attn_out, w_dist, b_dist = weights
    heads = w_bias.shape[1]
    bins = w_dist.shape[1]
    n_dev = n_row * n_col
    lanes = -(-tok * heads // 128) * 128
    group = rows // cols
    packed = cols * cols // 2
    b_dist = b_dist.reshape(1, bins)
    arrays = (pair, single, target_bins, token_pad, w_gate, w_up, w_out, w_bias, w_query, w_key, w_value, w_gating,
              w_attn_out, w_dist, b_dist)
    anywhere = pl.BlockSpec(memory_space=pl.ANY)
    vmem = pl.BlockSpec(memory_space=pltpu.VMEM)
    in_specs = [pl.BlockSpec(memory_space=pltpu.SMEM) if k == 3 else anywhere for k in range(len(arrays))]
    local = [pltpu.VMEM(a.shape, a.dtype) for k, a in enumerate(arrays) if k != 3]
    dma = pltpu.SemaphoreType.DMA
    return pl.pallas_call(
        functools.partial(kernel, n_row, n_col, heads),
        out_shape=(jax.ShapeDtypeStruct(pair.shape, F32), jax.ShapeDtypeStruct(single.shape, F32)),
        in_specs=in_specs,
        out_specs=(vmem, vmem),
        scratch_shapes=local + [
            pltpu.VMEM((tok, single_width + 128), F32),
            pltpu.VMEM((n_dev, tok, single_width + 128), F32),
            pltpu.VMEM((n_dev * tok, single_width + 128), F32),
            pltpu.VMEM((rows * cols, width), F32),
            pltpu.VMEM((rows * cols, bins), F32),
            pltpu.VMEM((group, cols, cols, bins), F32),
            pltpu.VMEM((group, packed + cols, 128), F32),
            pltpu.VMEM((group, packed + cols, 128), F32),
            pltpu.VMEM((n_col, cols, lanes), F32),
            pltpu.VMEM((n_col, cols, lanes), F32),
            dma((len(arrays) - 1,)), dma, dma, dma, dma, dma, dma,
        ],
        compiler_params=pltpu.CompilerParams(
            collective_id=0, has_side_effects=True, vmem_limit_bytes=56 * 2**20
        ),
        name="pairformer_close",
    )(*arrays)


def solution(mesh):
    in_specs = (
        P("row", "col", None),
        P(("row", "col"), None),
        P("row", "col"),
        P(("row", "col")),
    ) + (P(),) * 11
    out_specs = (P("row", "col", None), P(("row", "col"), None))
    body = functools.partial(per_device, mesh.shape["row"], mesh.shape["col"])
    return jax.shard_map(body, mesh=mesh, in_specs=in_specs, out_specs=out_specs, check_vma=False)
```

```python
import functools

import jax
import jax.numpy as jnp
from jax import lax
from jax.experimental import pallas as pl
from jax.experimental.pallas import tpu as pltpu
from jax.sharding import PartitionSpec as P

MESH = pl.DeviceIdType.MESH
F32 = jnp.float32
BF16 = jnp.bfloat16
NN = (((1,), (0,)), ((), ()))
NT = (((1,), (1,)), ((), ()))
PARTS = 2


def split(x):
    high = x.astype(BF16)
    return high, (x - high.astype(F32)).astype(BF16)


def mm(a, b, dims=NN):
    return lax.dot_general(a, b, dims, preferred_element_type=F32)


def dot3(a, b, dims=NN):
    ah, al = split(a)
    bh, bl = b if isinstance(b, tuple) else split(b)
    return mm(ah, bh, dims) + (mm(al, bh, dims) + mm(ah, bl, dims))


def layer_norm(x):
    mean = jnp.mean(x, axis=-1, keepdims=True)
    centred = x - mean
    var = jnp.mean(centred * centred, axis=-1, keepdims=True)
    return centred * lax.rsqrt(var + 1e-05)


def iota(shape, axis):
    return lax.broadcasted_iota(jnp.int32, shape, axis)


def kernel(n_row, n_col, heads, *refs):
    (pair_h, single_h, target_h, pad_s, gate_h, up_h, wout_h, wbias_h, wq_h, wk_h, wv_h, wg_h, wo_h, wdist_h, bdist_h,
     pair_o, single_o,
     pair_v, single_v, target_v, gate_v, up_v, wout_v, wbias_v, wq_v, wk_v, wv_v, wg_v, wo_v, wdist_v, bdist_v,
     ext, gath, tokens, mid_v, proj_v, flip_v, sbuf, rbuf, bsend, brecv,
     in_sem, g_send, g_recv, b_send, b_recv, p_send, p_recv) = refs
    rows, cols, width = pair_v.shape
    tok, single_width = single_v.shape
    bins = wdist_v.shape[0]
    group = rows // cols
    lanes = bsend.shape[2]
    head_dim = single_width // heads
    packed = cols * cols // 2
    r = lax.axis_index("row")
    c = lax.axis_index("col")

    sources = (single_h, pair_h, gate_h, up_h, wout_h, target_h, wbias_h, wdist_h, wk_h, wv_h, wq_h, wg_h, wo_h, bdist_h)
    targets = (single_v, pair_v, gate_v, up_v, wout_v, target_v, wbias_v, wdist_v, wk_v, wv_v, wq_v, wg_v, wo_v, bdist_v)
    loads = [pltpu.make_async_copy(a, b, in_sem.at[k]) for k, (a, b) in enumerate(zip(sources, targets))]
    for load in loads:
        load.start()

    chip, core = c // 2, lax.rem(c, 2)
    chips = n_col // 2
    p_row = c // group
    p_slot = lax.rem(c, group)
    at_home = p_row == r

    def is_self(k):
        return jnp.logical_and(at_home, p_slot == k)

    barrier = pltpu.get_barrier_semaphore()

    def greet(row, col):
        pl.semaphore_signal(barrier, inc=1, device_id=(row, col), device_id_type=MESH)

    for step in range(1, n_col):
        greet(r, lax.rem(c + step, n_col))
    for step in range(1, n_row):
        greet(lax.rem(r + step, n_row), c)

    @pl.when(jnp.logical_not(at_home))
    def _():
        for k in range(group):
            greet(p_row, group * r + k)

    loads[0].wait()
    row_id = iota((tok, 128), 0)
    pad_tile = jnp.zeros((tok, 128), F32)
    for q in range(tok):
        pad_tile = jnp.where(row_id == q, pad_s[q].astype(F32), pad_tile)
    ext[:, :single_width] = single_v[...]
    ext[:, single_width:] = pad_tile
    gath[chip, core, r] = ext[...]
    pl.semaphore_wait(barrier, n_col + n_row - 2 + jnp.where(at_home, 0, group))

    for step in range(1, n_row):
        pltpu.make_async_remote_copy(ext, gath.at[chip, core, r], g_send.at[0], g_recv.at[0], device_id=(lax.rem(r + step, n_row), c), device_id_type=MESH).start()

    for load in loads[1:8]:
        load.wait()

    gate_w = split(gate_v[...])
    up_w = split(up_v[...])
    out_w = split(wout_v[...])
    wdist = wdist_v[...]
    dist_w = split(wdist)
    none = jnp.zeros_like(wdist)
    wide = jnp.concatenate([jnp.concatenate([wdist, none], axis=1), jnp.concatenate([none, wdist], axis=1)], axis=0)
    wide_w = split(wide)
    slots = lanes // heads
    bias_rep = jnp.concatenate([wbias_v[...]] * slots, axis=0)
    row_q = iota((lanes, width), 0) // heads
    bias_w = split(jnp.concatenate([jnp.where(row_q == q, bias_rep, 0.0) for q in range(tok)], axis=1))

    bin_rows = target_v[...].astype(F32)
    eye = (iota((rows, rows), 0) == iota((rows, rows), 1)).astype(BF16)
    filled = jnp.concatenate([bin_rows, jnp.zeros((128 - cols, rows), F32)], axis=0).astype(BF16)
    sbuf[:, packed:, :] = mm(eye, filled, NT).reshape(group, cols, 128)

    def drain(ref, sem):
        pltpu.make_async_copy(ref, ref, sem).wait()

    drain(gath.at[0, 0, pl.ds(0, n_row - 1)], g_recv.at[0])
    for step in range(1, chips):
        pltpu.make_async_remote_copy(gath.at[chip, core], gath.at[chip, core], g_send.at[1], g_recv.at[1], device_id=(r, lax.rem(c + 2 * step, n_col)), device_id_type=MESH).start()

    part = rows // PARTS

    def send_bias(d, carry):
        @pl.when(d != c)
        def _():
            pltpu.make_async_remote_copy(bsend.at[d], brecv.at[c], b_send, b_recv, device_id=(r, d), device_id_type=MESH).start()
        return carry

    def send_proj(k, carry):
        @pl.when(jnp.logical_not(is_self(k)))
        def _():
            pltpu.make_async_remote_copy(sbuf.at[k], rbuf.at[p_slot], p_send, p_recv, device_id=(p_row, group * r + k), device_id_type=MESH).start()
        return carry

    for s in range(PARTS):
        first = s * part
        x = pair_v[first:first + part].reshape(part * cols, width)
        normed = layer_norm(x)
        g = dot3(normed, gate_w)
        u = dot3(normed, up_w)
        hidden = g / (1.0 + jnp.exp(-g)) * u
        mid = x + dot3(hidden, out_w)
        mid_v[first * cols:(first + part) * cols] = mid
        tiles = part // cols
        halves = mid.reshape(tiles, 2, packed, width)
        both = jnp.concatenate([halves[:, 0].reshape(tiles * packed, width), halves[:, 1].reshape(tiles * packed, width)], axis=1)
        k0 = first // cols
        sbuf[k0:k0 + tiles, :packed, :] = dot3(both, wide_w, NT).reshape(tiles, packed, 2 * bins)
        lax.fori_loop(k0, k0 + tiles, send_proj, 0)
        dests = part // tok
        norm_mid = layer_norm(mid).reshape(dests, tok, cols, width)
        quad = jnp.concatenate([norm_mid[:, q].reshape(dests * cols, width) for q in range(tok)], axis=1)
        d0 = first // tok
        bsend[d0:d0 + dests] = dot3(quad, bias_w, NT).reshape(dests, cols, lanes)
        lax.fori_loop(d0, d0 + dests, send_bias, 0)
        proj_v[first * cols:(first + part) * cols] = dot3(mid, dist_w, NT)
        if s == 0:
            drain(gath.at[pl.ds(0, chips - 1), 0], g_recv.at[1])
            pltpu.make_async_remote_copy(gath.at[:, core], gath.at[:, core], g_send.at[2], g_recv.at[2], device_id=(r, c + 1 - 2 * core), device_id_type=MESH).start()

    brecv[c] = bsend[c]

    @pl.when(p_row == r)
    def _():
        rbuf[p_slot] = sbuf[p_slot]

    for load in loads[8:]:
        load.wait()

    drain(gath.at[:, 0], g_recv.at[2])
    step = 8 // tok
    for row in range(n_row):
        for m in range(0, n_col, step):
            at = (row * n_col + m) * tok
            tokens[at:at + 8, :] = jnp.concatenate([gath[(m + q) // 2, (m + q) % 2, row] for q in range(step)], axis=0)
    everyone = layer_norm(tokens[:, :single_width])
    key = dot3(everyone, wk_v[...])
    value = dot3(everyone, wv_v[...])
    own = jnp.concatenate([single_v[...], jnp.zeros((slots - tok, single_width), F32)], axis=0)
    own_norm = layer_norm(own)
    query = dot3(own_norm, wq_v[...])
    gating = jax.nn.sigmoid(dot3(own_norm, wg_v[...]))
    head_mask = (iota((heads, single_width), 1) // head_dim == iota((heads, single_width), 0)).astype(F32)
    query_wide = (query[:, None, :] * head_mask[None]).reshape(lanes, single_width)
    scores = dot3(key, query_wide, NT) * (1.0 / head_dim ** 0.5)
    pads = tokens[:, single_width:]

    drain(brecv.at[pl.ds(0, n_col - 1)], b_recv)
    scores = scores + brecv[...].reshape(scores.shape)
    scores = jnp.where(pads > 0.5, scores, -1e9)
    expo = jnp.exp(scores - jnp.max(scores, axis=0, keepdims=True))
    weights = expo / jnp.sum(expo, axis=0, keepdims=True)
    mixed = dot3(jnp.transpose(weights), value).reshape(slots, heads, single_width)
    attended = jnp.sum(mixed * head_mask[None], axis=1)
    single_o[...] = (own + dot3(gating * attended, wo_v[...]))[:tok]

    @pl.when(p_row == r)
    def _():
        drain(rbuf.at[pl.ds(0, group - 1)], p_recv)

    @pl.when(p_row != r)
    def _():
        drain(rbuf, p_recv)

    half = cols // 2
    for q in range(cols):
        piece = rbuf[:, pl.ds(q, half, stride=cols), :]
        flip_v[:, q] = jnp.concatenate([piece[:, :, :bins], piece[:, :, bins:]], axis=1)
    total = rows * cols
    logits = proj_v[...] + flip_v[...].reshape(total, bins) + bdist_v[...]
    expo = jnp.exp(logits - jnp.max(logits, axis=-1, keepdims=True))
    probs = expo / jnp.sum(expo, axis=-1, keepdims=True)
    ones = jnp.ones((cols, bins), BF16)
    three = (rows, cols, rows)
    mine = jnp.where(iota(three, 2) == iota(three, 0), jnp.broadcast_to(bin_rows[None], three), 0.0).reshape(total, rows)
    mine = mm(mine.astype(BF16), jnp.ones((rows, bins), BF16))
    theirs = jnp.broadcast_to(rbuf[:, packed:, :cols][:, None], (group, cols, cols, cols))
    fours = (group, cols, cols, cols)
    theirs = jnp.where(iota(fours, 3) == iota(fours, 1), theirs, 0.0).reshape(total, cols)
    theirs = mm(theirs.astype(BF16), ones)
    bin_id = iota((total, bins), 1).astype(F32)
    hot = (mine == bin_id).astype(F32) + (theirs == bin_id).astype(F32)
    pad_i = tokens[pl.ds(pl.multiple_of(r * rows, rows), rows), single_width:single_width + bins]
    pad_j = tokens[pl.ds(pl.multiple_of(c * cols, cols), cols), single_width:single_width + bins]
    mask = (pad_i[:, None, :] * pad_j[None, :, :]).reshape(total, bins)
    delta = mask * (2.0 * probs - hot)
    pair_o[...] = (mid_v[...] + dot3(delta, dist_w)).reshape(rows, cols, width)

    drain(gath.at[0, 0, pl.ds(0, n_row - 1)], g_send.at[0])
    drain(gath.at[pl.ds(0, chips - 1), 0], g_send.at[1])
    drain(gath.at[:, 0], g_send.at[2])
    drain(brecv.at[pl.ds(0, n_col - 1)], b_send)

    @pl.when(p_row == r)
    def _():
        drain(rbuf.at[pl.ds(0, group - 1)], p_send)

    @pl.when(p_row != r)
    def _():
        drain(rbuf, p_send)


def per_device(n_row, n_col, pair, single, target_bins, token_pad, *weights):
    rows, cols, width = pair.shape
    tok, single_width = single.shape
    w_gate, w_up, w_out, w_bias, w_query, w_key, w_value, w_gating, w_attn_out, w_dist, b_dist = weights
    heads = w_bias.shape[1]
    bins = w_dist.shape[1]
    w_bias, w_dist, target_bins = w_bias.T, w_dist.T, target_bins.T
    n_dev = n_row * n_col
    lanes = -(-tok * heads // 128) * 128
    group = rows // cols
    packed = cols * cols // 2
    b_dist = b_dist.reshape(1, bins)
    arrays = (pair, single, target_bins, token_pad, w_gate, w_up, w_out, w_bias, w_query, w_key, w_value, w_gating,
              w_attn_out, w_dist, b_dist)
    anywhere = pl.BlockSpec(memory_space=pl.ANY)
    vmem = pl.BlockSpec(memory_space=pltpu.VMEM)
    in_specs = [pl.BlockSpec(memory_space=pltpu.SMEM) if k == 3 else anywhere for k in range(len(arrays))]
    local = [pltpu.VMEM(a.shape, a.dtype) for k, a in enumerate(arrays) if k != 3]
    dma = pltpu.SemaphoreType.DMA
    return pl.pallas_call(
        functools.partial(kernel, n_row, n_col, heads),
        out_shape=(jax.ShapeDtypeStruct(pair.shape, F32), jax.ShapeDtypeStruct(single.shape, F32)),
        in_specs=in_specs,
        out_specs=(vmem, vmem),
        scratch_shapes=local + [
            pltpu.VMEM((tok, single_width + 128), F32),
            pltpu.VMEM((n_col // 2, 2, n_row, tok, single_width + 128), F32),
            pltpu.VMEM((n_dev * tok, single_width + 128), F32),
            pltpu.VMEM((rows * cols, width), F32),
            pltpu.VMEM((rows * cols, bins), F32),
            pltpu.VMEM((group, cols, cols, bins), F32),
            pltpu.VMEM((group, packed + cols, 128), F32),
            pltpu.VMEM((group, packed + cols, 128), F32),
            pltpu.VMEM((n_col, cols, lanes), F32),
            pltpu.VMEM((n_col, cols, lanes), F32),
            dma((len(arrays) - 1,)), dma((3,)), dma((3,)), dma, dma, dma, dma,
        ],
        compiler_params=pltpu.CompilerParams(
            collective_id=0, has_side_effects=True, vmem_limit_bytes=56 * 2**20
        ),
        name="pairformer_close",
    )(*arrays)


def solution(mesh):
    in_specs = (
        P("row", "col", None),
        P(("row", "col"), None),
        P("row", "col"),
        P(("row", "col")),
    ) + (P(),) * 11
    out_specs = (P("row", "col", None), P(("row", "col"), None))
    body = functools.partial(per_device, mesh.shape["row"], mesh.shape["col"])
    return jax.shard_map(body, mesh=mesh, in_specs=in_specs, out_specs=out_specs, check_vma=False)
```

```python
import functools

import jax
import jax.numpy as jnp
from jax import lax
from jax.experimental import pallas as pl
from jax.experimental.pallas import tpu as pltpu
from jax.sharding import PartitionSpec as P

MESH = pl.DeviceIdType.MESH
F32 = jnp.float32
BF16 = jnp.bfloat16
NN = (((1,), (0,)), ((), ()))
NT = (((1,), (1,)), ((), ()))
PARTS = 2


def split(x):
    high = x.astype(BF16)
    return high, (x - high.astype(F32)).astype(BF16)


def mm(a, b, dims=NN):
    return lax.dot_general(a, b, dims, preferred_element_type=F32)


def dot3(a, b, dims=NN):
    ah, al = split(a)
    bh, bl = b if isinstance(b, tuple) else split(b)
    rows = a.shape[0]
    if rows % 16:
        both = mm(jnp.concatenate([ah.astype(F32), al.astype(F32)], axis=0).astype(BF16), bh, dims)
    else:
        both = mm(jnp.concatenate([ah, al], axis=0), bh, dims)
    return both[:rows] + (both[rows:] + mm(ah, bl, dims))


def layer_norm(x):
    mean = jnp.mean(x, axis=-1, keepdims=True)
    centred = x - mean
    var = jnp.mean(centred * centred, axis=-1, keepdims=True)
    return centred * lax.rsqrt(var + 1e-05)


def iota(shape, axis):
    return lax.broadcasted_iota(jnp.int32, shape, axis)


def kernel(n_row, n_col, heads, *refs):
    (pair_h, single_h, target_h, pad_s, gate_h, up_h, wout_h, wbias_h, wq_h, wk_h, wv_h, wg_h, wo_h, wdist_h, bdist_h,
     pair_o, single_o,
     pair_v, single_v, target_v, gate_v, up_v, wout_v, wbias_v, wq_v, wk_v, wv_v, wg_v, wo_v, wdist_v, bdist_v,
     ext, gath, tokens, mid_v, proj_v, flip_v, sbuf, rbuf, bsend, brecv,
     in_sem, g_send, g_recv, b_send, b_recv, p_send, p_recv) = refs
    rows, cols, width = pair_v.shape
    tok, single_width = single_v.shape
    bins = wdist_v.shape[0]
    group = rows // cols
    lanes = bsend.shape[2]
    head_dim = single_width // heads
    packed = cols * cols // 2
    r = lax.axis_index("row")
    c = lax.axis_index("col")

    sources = (single_h, pair_h, gate_h, up_h, wout_h, target_h, wbias_h, wdist_h, wk_h, wv_h, wq_h, wg_h, wo_h, bdist_h)
    targets = (single_v, pair_v, gate_v, up_v, wout_v, target_v, wbias_v, wdist_v, wk_v, wv_v, wq_v, wg_v, wo_v, bdist_v)
    loads = [pltpu.make_async_copy(a, b, in_sem.at[k]) for k, (a, b) in enumerate(zip(sources, targets))]
    for load in loads:
        load.start()

    chip, core = c // 2, lax.rem(c, 2)
    chips = n_col // 2
    p_row = c // group
    p_slot = lax.rem(c, group)
    at_home = p_row == r

    def is_self(k):
        return jnp.logical_and(at_home, p_slot == k)

    barrier = pltpu.get_barrier_semaphore()

    def greet(row, col):
        pl.semaphore_signal(barrier, inc=1, device_id=(row, col), device_id_type=MESH)

    for step in range(1, n_col):
        greet(r, lax.rem(c + step, n_col))
    for step in range(1, n_row):
        greet(lax.rem(r + step, n_row), c)

    @pl.when(jnp.logical_not(at_home))
    def _():
        for k in range(group):
            greet(p_row, group * r + k)

    loads[0].wait()
    row_id = iota((tok, 128), 0)
    pad_tile = jnp.zeros((tok, 128), F32)
    for q in range(tok):
        pad_tile = jnp.where(row_id == q, pad_s[q].astype(F32), pad_tile)
    ext[:, :single_width] = single_v[...]
    ext[:, single_width:] = pad_tile
    gath[chip, core, r] = ext[...]
    pl.semaphore_wait(barrier, n_col + n_row - 2 + jnp.where(at_home, 0, group))

    for step in range(1, n_row):
        pltpu.make_async_remote_copy(ext, gath.at[chip, core, r], g_send.at[0], g_recv.at[0], device_id=(lax.rem(r + step, n_row), c), device_id_type=MESH).start()

    for load in loads[1:8]:
        load.wait()

    gate_w = split(gate_v[...])
    up_w = split(up_v[...])
    out_w = split(wout_v[...])
    wdist = wdist_v[...]
    dist_w = split(wdist)
    none = jnp.zeros_like(wdist)
    wide = jnp.concatenate([jnp.concatenate([wdist, none], axis=1), jnp.concatenate([none, wdist], axis=1)], axis=0)
    wide_w = split(wide)
    slots = lanes // heads
    bias_rep = jnp.concatenate([wbias_v[...]] * slots, axis=0)
    row_q = iota((lanes, width), 0) // heads
    bias_w = split(jnp.concatenate([jnp.where(row_q == q, bias_rep, 0.0) for q in range(tok)], axis=1))

    bin_rows = target_v[...].astype(F32)
    eye = (iota((rows, rows), 0) == iota((rows, rows), 1)).astype(BF16)
    filled = jnp.concatenate([bin_rows, jnp.zeros((128 - cols, rows), F32)], axis=0).astype(BF16)
    sbuf[:, packed:, :] = mm(eye, filled, NT).reshape(group, cols, 128)

    def drain(ref, sem):
        pltpu.make_async_copy(ref, ref, sem).wait()

    drain(gath.at[0, 0, pl.ds(0, n_row - 1)], g_recv.at[0])
    for step in range(1, chips):
        pltpu.make_async_remote_copy(gath.at[chip, core], gath.at[chip, core], g_send.at[1], g_recv.at[1], device_id=(r, lax.rem(c + 2 * step, n_col)), device_id_type=MESH).start()

    part = rows // PARTS

    def send_bias(d, carry):
        @pl.when(d != c)
        def _():
            pltpu.make_async_remote_copy(bsend.at[d], brecv.at[c], b_send, b_recv, device_id=(r, d), device_id_type=MESH).start()
        return carry

    def send_proj(k, carry):
        @pl.when(jnp.logical_not(is_self(k)))
        def _():
            pltpu.make_async_remote_copy(sbuf.at[k], rbuf.at[p_slot], p_send, p_recv, device_id=(p_row, group * r + k), device_id_type=MESH).start()
        return carry

    for s in range(PARTS):
        first = s * part
        x = pair_v[first:first + part].reshape(part * cols, width)
        normed = layer_norm(x)
        g = dot3(normed, gate_w)
        u = dot3(normed, up_w)
        hidden = g / (1.0 + jnp.exp(-g)) * u
        mid = x + dot3(hidden, out_w)
        mid_v[first * cols:(first + part) * cols] = mid
        tiles = part // cols
        halves = mid.reshape(tiles, 2, packed, width)
        both = jnp.concatenate([halves[:, 0].reshape(tiles * packed, width), halves[:, 1].reshape(tiles * packed, width)], axis=1)
        k0 = first // cols
        sbuf[k0:k0 + tiles, :packed, :] = dot3(both, wide_w, NT).reshape(tiles, packed, 2 * bins)
        lax.fori_loop(k0, k0 + tiles, send_proj, 0)
        dests = part // tok
        norm_mid = layer_norm(mid).reshape(dests, tok, cols, width)
        quad = jnp.concatenate([norm_mid[:, q].reshape(dests * cols, width) for q in range(tok)], axis=1)
        d0 = first // tok
        bsend[d0:d0 + dests] = dot3(quad, bias_w, NT).reshape(dests, cols, lanes)
        lax.fori_loop(d0, d0 + dests, send_bias, 0)
        proj_v[first * cols:(first + part) * cols] = dot3(mid, dist_w, NT)
        if s == 0:
            drain(gath.at[pl.ds(0, chips - 1), 0], g_recv.at[1])
            pltpu.make_async_remote_copy(gath.at[:, core], gath.at[:, core], g_send.at[2], g_recv.at[2], device_id=(r, c + 1 - 2 * core), device_id_type=MESH).start()

    brecv[c] = bsend[c]

    @pl.when(p_row == r)
    def _():
        rbuf[p_slot] = sbuf[p_slot]

    for load in loads[8:]:
        load.wait()

    drain(gath.at[:, 0], g_recv.at[2])
    step = 8 // tok
    for row in range(n_row):
        for m in range(0, n_col, step):
            at = (row * n_col + m) * tok
            tokens[at:at + 8, :] = jnp.concatenate([gath[(m + q) // 2, (m + q) % 2, row] for q in range(step)], axis=0)
    everyone = layer_norm(tokens[:, :single_width])
    key = dot3(everyone, wk_v[...])
    value = dot3(everyone, wv_v[...])
    own = jnp.concatenate([single_v[...], jnp.zeros((slots - tok, single_width), F32)], axis=0)
    own_norm = layer_norm(own)
    query = dot3(own_norm, wq_v[...])
    gating = jax.nn.sigmoid(dot3(own_norm, wg_v[...]))
    head_mask = (iota((heads, single_width), 1) // head_dim == iota((heads, single_width), 0)).astype(F32)
    query_wide = (query[:, None, :] * head_mask[None]).reshape(lanes, single_width)
    scores = dot3(key, query_wide, NT) * (1.0 / head_dim ** 0.5)
    pads = tokens[:, single_width:]

    drain(brecv.at[pl.ds(0, n_col - 1)], b_recv)
    scores = scores + brecv[...].reshape(scores.shape)
    scores = jnp.where(pads > 0.5, scores, -1e9)
    expo = jnp.exp(scores - jnp.max(scores, axis=0, keepdims=True))
    weights = expo / jnp.sum(expo, axis=0, keepdims=True)
    mixed = dot3(jnp.transpose(weights), value).reshape(slots, heads, single_width)
    attended = jnp.sum(mixed * head_mask[None], axis=1)
    single_o[...] = (own + dot3(gating * attended, wo_v[...]))[:tok]

    @pl.when(p_row == r)
    def _():
        drain(rbuf.at[pl.ds(0, group - 1)], p_recv)

    @pl.when(p_row != r)
    def _():
        drain(rbuf, p_recv)

    half = cols // 2
    for q in range(cols):
        piece = rbuf[:, pl.ds(q, half, stride=cols), :]
        flip_v[:, q] = jnp.concatenate([piece[:, :, :bins], piece[:, :, bins:]], axis=1)
    total = rows * cols
    logits = proj_v[...] + flip_v[...].reshape(total, bins) + bdist_v[...]
    expo = jnp.exp(logits - jnp.max(logits, axis=-1, keepdims=True))
    probs = expo / jnp.sum(expo, axis=-1, keepdims=True)
    ones = jnp.ones((cols, bins), BF16)
    three = (rows, cols, rows)
    mine = jnp.where(iota(three, 2) == iota(three, 0), jnp.broadcast_to(bin_rows[None], three), 0.0).reshape(total, rows)
    mine = mm(mine.astype(BF16), jnp.ones((rows, bins), BF16))
    theirs = jnp.broadcast_to(rbuf[:, packed:, :cols][:, None], (group, cols, cols, cols))
    fours = (group, cols, cols, cols)
    theirs = jnp.where(iota(fours, 3) == iota(fours, 1), theirs, 0.0).reshape(total, cols)
    theirs = mm(theirs.astype(BF16), ones)
    bin_id = iota((total, bins), 1).astype(F32)
    hot = (mine == bin_id).astype(F32) + (theirs == bin_id).astype(F32)
    pad_i = tokens[pl.ds(pl.multiple_of(r * rows, rows), rows), single_width:single_width + bins]
    pad_j = tokens[pl.ds(pl.multiple_of(c * cols, cols), cols), single_width:single_width + bins]
    mask = (pad_i[:, None, :] * pad_j[None, :, :]).reshape(total, bins)
    delta = mask * (2.0 * probs - hot)
    pair_o[...] = (mid_v[...] + dot3(delta, dist_w)).reshape(rows, cols, width)

    drain(gath.at[0, 0, pl.ds(0, n_row - 1)], g_send.at[0])
    drain(gath.at[pl.ds(0, chips - 1), 0], g_send.at[1])
    drain(gath.at[:, 0], g_send.at[2])
    drain(brecv.at[pl.ds(0, n_col - 1)], b_send)

    @pl.when(p_row == r)
    def _():
        drain(rbuf.at[pl.ds(0, group - 1)], p_send)

    @pl.when(p_row != r)
    def _():
        drain(rbuf, p_send)


def hand_over(pair_in, single_in, pair_out, single_out, pair_sem, single_sem):
    first = pltpu.make_async_copy(pair_in, pair_out, pair_sem)
    second = pltpu.make_async_copy(single_in, single_out, single_sem)
    first.start()
    second.start()
    first.wait()
    second.wait()


def per_device(n_row, n_col, pair, single, target_bins, token_pad, *weights):
    rows, cols, width = pair.shape
    tok, single_width = single.shape
    w_gate, w_up, w_out, w_bias, w_query, w_key, w_value, w_gating, w_attn_out, w_dist, b_dist = weights
    heads = w_bias.shape[1]
    bins = w_dist.shape[1]
    w_bias, w_dist, target_bins = w_bias.T, w_dist.T, target_bins.T
    n_dev = n_row * n_col
    lanes = -(-tok * heads // 128) * 128
    group = rows // cols
    packed = cols * cols // 2
    b_dist = b_dist.reshape(1, bins)
    arrays = (pair, single, target_bins, token_pad, w_gate, w_up, w_out, w_bias, w_query, w_key, w_value, w_gating,
              w_attn_out, w_dist, b_dist)
    anywhere = pl.BlockSpec(memory_space=pl.ANY)
    vmem = pl.BlockSpec(memory_space=pltpu.VMEM)
    in_specs = [pl.BlockSpec(memory_space=pltpu.SMEM) if k == 3 else anywhere for k in range(len(arrays))]
    local = [pltpu.VMEM(a.shape, a.dtype) for k, a in enumerate(arrays) if k != 3]
    dma = pltpu.SemaphoreType.DMA
    results = pl.pallas_call(
        functools.partial(kernel, n_row, n_col, heads),
        out_shape=(pltpu.VMEM(pair.shape, F32), pltpu.VMEM(single.shape, F32)),
        in_specs=in_specs,
        out_specs=(vmem, vmem),
        scratch_shapes=local + [
            pltpu.VMEM((tok, single_width + 128), F32),
            pltpu.VMEM((n_col // 2, 2, n_row, tok, single_width + 128), F32),
            pltpu.VMEM((n_dev * tok, single_width + 128), F32),
            pltpu.VMEM((rows * cols, width), F32),
            pltpu.VMEM((rows * cols, bins), F32),
            pltpu.VMEM((group, cols, cols, bins), F32),
            pltpu.VMEM((group, packed + cols, 128), F32),
            pltpu.VMEM((group, packed + cols, 128), F32),
            pltpu.VMEM((n_col, cols, lanes), F32),
            pltpu.VMEM((n_col, cols, lanes), F32),
            dma((len(arrays) - 1,)), dma((3,)), dma((3,)), dma, dma, dma, dma,
        ],
        compiler_params=pltpu.CompilerParams(
            collective_id=0, has_side_effects=True, vmem_limit_bytes=56 * 2**20
        ),
        name="pairformer_close",
    )(*arrays)
    return pl.pallas_call(
        hand_over,
        out_shape=(jax.ShapeDtypeStruct(pair.shape, F32), jax.ShapeDtypeStruct(single.shape, F32)),
        in_specs=[vmem, vmem],
        out_specs=(anywhere, anywhere),
        scratch_shapes=[dma, dma],
        name="hand_over",
    )(*results)


def solution(mesh):
    in_specs = (
        P("row", "col", None),
        P(("row", "col"), None),
        P("row", "col"),
        P(("row", "col")),
    ) + (P(),) * 11
    out_specs = (P("row", "col", None), P(("row", "col"), None))
    body = functools.partial(per_device, mesh.shape["row"], mesh.shape["col"])
    return jax.shard_map(body, mesh=mesh, in_specs=in_specs, out_specs=out_specs, check_vma=False)
```

```python
import functools

import jax
import jax.numpy as jnp
from jax import lax
from jax.experimental import pallas as pl
from jax.experimental.pallas import tpu as pltpu
from jax.sharding import PartitionSpec as P

MESH = pl.DeviceIdType.MESH
F32 = jnp.float32
BF16 = jnp.bfloat16
NN = (((1,), (0,)), ((), ()))
NT = (((1,), (1,)), ((), ()))
PARTS = 4


def split(x):
    high = x.astype(BF16)
    return high, (x - high.astype(F32)).astype(BF16)


def mm(a, b, dims=NN):
    return lax.dot_general(a, b, dims, preferred_element_type=F32)


def dot3(a, b, dims=NN):
    ah, al = split(a)
    bh, bl = b if isinstance(b, tuple) else split(b)
    rows = a.shape[0]
    if rows % 16:
        both = mm(jnp.concatenate([ah.astype(F32), al.astype(F32)], axis=0).astype(BF16), bh, dims)
    else:
        both = mm(jnp.concatenate([ah, al], axis=0), bh, dims)
    return both[:rows] + (both[rows:] + mm(ah, bl, dims))


def layer_norm(x):
    mean = jnp.mean(x, axis=-1, keepdims=True)
    centred = x - mean
    var = jnp.mean(centred * centred, axis=-1, keepdims=True)
    return centred * lax.rsqrt(var + 1e-05)


def iota(shape, axis):
    return lax.broadcasted_iota(jnp.int32, shape, axis)


def kernel(n_row, n_col, heads, *refs):
    (pair_h, single_h, target_h, pad_s, gate_h, up_h, wout_h, wbias_h, wq_h, wk_h, wv_h, wg_h, wo_h, wdist_h, bdist_h,
     pair_o, single_o,
     pair_v, single_v, target_v, gate_v, up_v, wout_v, wbias_v, wq_v, wk_v, wv_v, wg_v, wo_v, wdist_v, bdist_v,
     ext, gath, tokens, mid_v, proj_v, flip_v, sbuf, rbuf, bsend, brecv,
     in_sem, g_send, g_recv, b_send, b_recv, p_send, p_recv) = refs
    rows, cols, width = pair_v.shape
    tok, single_width = single_v.shape
    bins = wdist_v.shape[0]
    group = rows // cols
    lanes = bsend.shape[2]
    head_dim = single_width // heads
    packed = cols * cols // 2
    r = lax.axis_index("row")
    c = lax.axis_index("col")

    sources = (single_h, pair_h, gate_h, up_h, wout_h, target_h, wbias_h, wdist_h, wk_h, wv_h, wq_h, wg_h, wo_h, bdist_h)
    targets = (single_v, pair_v, gate_v, up_v, wout_v, target_v, wbias_v, wdist_v, wk_v, wv_v, wq_v, wg_v, wo_v, bdist_v)
    loads = [pltpu.make_async_copy(a, b, in_sem.at[k]) for k, (a, b) in enumerate(zip(sources, targets))]
    for load in loads:
        load.start()

    chip, core = c // 2, lax.rem(c, 2)
    chips = n_col // 2
    p_row = c // group
    p_slot = lax.rem(c, group)
    at_home = p_row == r

    def is_self(k):
        return jnp.logical_and(at_home, p_slot == k)

    barrier = pltpu.get_barrier_semaphore()

    def greet(row, col):
        pl.semaphore_signal(barrier, inc=1, device_id=(row, col), device_id_type=MESH)

    for step in range(1, n_col):
        greet(r, lax.rem(c + step, n_col))
    for step in range(1, n_row):
        greet(lax.rem(r + step, n_row), c)

    @pl.when(jnp.logical_not(at_home))
    def _():
        for k in range(group):
            greet(p_row, group * r + k)

    loads[0].wait()
    row_id = iota((tok, 128), 0)
    pad_tile = jnp.zeros((tok, 128), F32)
    for q in range(tok):
        pad_tile = jnp.where(row_id == q, pad_s[q].astype(F32), pad_tile)
    ext[:, :single_width] = single_v[...]
    ext[:, single_width:] = pad_tile
    gath[chip, core, r] = ext[...]
    pl.semaphore_wait(barrier, n_col + n_row - 2 + jnp.where(at_home, 0, group))

    for step in range(1, n_row):
        pltpu.make_async_remote_copy(ext, gath.at[chip, core, r], g_send.at[0], g_recv.at[0], device_id=(lax.rem(r + step, n_row), c), device_id_type=MESH).start()

    for load in loads[1:8]:
        load.wait()

    gate_w = split(gate_v[...])
    up_w = split(up_v[...])
    out_w = split(wout_v[...])
    wdist = wdist_v[...]
    dist_w = split(wdist)
    none = jnp.zeros_like(wdist)
    wide = jnp.concatenate([jnp.concatenate([wdist, none], axis=1), jnp.concatenate([none, wdist], axis=1)], axis=0)
    wide_w = split(wide)
    slots = lanes // heads
    bias_rep = jnp.concatenate([wbias_v[...]] * slots, axis=0)
    row_q = iota((lanes, width), 0) // heads
    bias_w = split(jnp.concatenate([jnp.where(row_q == q, bias_rep, 0.0) for q in range(tok)], axis=1))

    bin_rows = target_v[...].astype(F32)
    eye = (iota((rows, rows), 0) == iota((rows, rows), 1)).astype(BF16)
    filled = jnp.concatenate([bin_rows, jnp.zeros((128 - cols, rows), F32)], axis=0).astype(BF16)
    sbuf[:, packed:, :] = mm(eye, filled, NT).reshape(group, cols, 128)

    def drain(ref, sem):
        pltpu.make_async_copy(ref, ref, sem).wait()

    part = rows // PARTS

    def send_bias(d, carry):
        @pl.when(d != c)
        def _():
            pltpu.make_async_remote_copy(bsend.at[d], brecv.at[c], b_send, b_recv, device_id=(r, d), device_id_type=MESH).start()
        return carry

    def send_proj(k, carry):
        @pl.when(jnp.logical_not(is_self(k)))
        def _():
            pltpu.make_async_remote_copy(sbuf.at[k], rbuf.at[p_slot], p_send, p_recv, device_id=(p_row, group * r + k), device_id_type=MESH).start()
        return carry

    for s in range(PARTS):
        first = s * part
        x = pair_v[first:first + part].reshape(part * cols, width)
        normed = layer_norm(x)
        g = dot3(normed, gate_w)
        u = dot3(normed, up_w)
        hidden = g / (1.0 + jnp.exp(-g)) * u
        change = dot3(hidden, out_w)
        pair_o[first * cols:(first + part) * cols] = change
        mid = x + change
        mid_v[first * cols:(first + part) * cols] = mid
        tiles = part // cols
        halves = mid.reshape(tiles, 2, packed, width)
        both = jnp.concatenate([halves[:, 0].reshape(tiles * packed, width), halves[:, 1].reshape(tiles * packed, width)], axis=1)
        k0 = first // cols
        sbuf[k0:k0 + tiles, :packed, :] = dot3(both, wide_w, NT).reshape(tiles, packed, 2 * bins)
        lax.fori_loop(k0, k0 + tiles, send_proj, 0)
        dests = part // tok
        norm_mid = layer_norm(mid).reshape(dests, tok, cols, width)
        quad = jnp.concatenate([norm_mid[:, q].reshape(dests * cols, width) for q in range(tok)], axis=1)
        d0 = first // tok
        bsend[d0:d0 + dests] = dot3(quad, bias_w, NT).reshape(dests, cols, lanes)
        lax.fori_loop(d0, d0 + dests, send_bias, 0)
        if s == 0:
            drain(gath.at[0, 0, pl.ds(0, n_row - 1)], g_recv.at[0])
            for step in range(1, chips):
                pltpu.make_async_remote_copy(gath.at[chip, core], gath.at[chip, core], g_send.at[1], g_recv.at[1], device_id=(r, lax.rem(c + 2 * step, n_col)), device_id_type=MESH).start()
        if s == PARTS // 2:
            drain(gath.at[pl.ds(0, chips - 1), 0], g_recv.at[1])
            pltpu.make_async_remote_copy(gath.at[:, core], gath.at[:, core], g_send.at[2], g_recv.at[2], device_id=(r, c + 1 - 2 * core), device_id_type=MESH).start()

    brecv[c] = bsend[c]

    @pl.when(p_row == r)
    def _():
        rbuf[p_slot] = sbuf[p_slot]

    for load in loads[8:]:
        load.wait()

    own = jnp.concatenate([single_v[...], jnp.zeros((slots - tok, single_width), F32)], axis=0)
    own_norm = layer_norm(own)
    query = dot3(own_norm, wq_v[...])
    gating = jax.nn.sigmoid(dot3(own_norm, wg_v[...]))
    total = rows * cols
    proj_v[...] = dot3(mid_v[...], dist_w, NT)
    ones = jnp.ones((cols, bins), BF16)
    three = (rows, cols, rows)
    mine = jnp.where(iota(three, 2) == iota(three, 0), jnp.broadcast_to(bin_rows[None], three), 0.0).reshape(total, rows)
    mine = mm(mine.astype(BF16), jnp.ones((rows, bins), BF16))
    drain(gath.at[:, 0], g_recv.at[2])
    step = 8 // tok
    for row in range(n_row):
        for m in range(0, n_col, step):
            at = (row * n_col + m) * tok
            tokens[at:at + 8, :] = jnp.concatenate([gath[(m + q) // 2, (m + q) % 2, row] for q in range(step)], axis=0)
    everyone = layer_norm(tokens[:, :single_width])
    key = dot3(everyone, wk_v[...])
    value = dot3(everyone, wv_v[...])
    head_mask = (iota((heads, single_width), 1) // head_dim == iota((heads, single_width), 0)).astype(F32)
    query_wide = (query[:, None, :] * head_mask[None]).reshape(lanes, single_width)
    scores = dot3(key, query_wide, NT) * (1.0 / head_dim ** 0.5)
    pads = tokens[:, single_width:]

    drain(brecv.at[pl.ds(0, n_col - 1)], b_recv)
    scores = scores + brecv[...].reshape(scores.shape)
    scores = jnp.where(pads > 0.5, scores, -1e9)
    expo = jnp.exp(scores - jnp.max(scores, axis=0, keepdims=True))
    weights = expo / jnp.sum(expo, axis=0, keepdims=True)
    mixed = dot3(jnp.transpose(weights), value).reshape(slots, heads, single_width)
    attended = jnp.sum(mixed * head_mask[None], axis=1)
    single_o[...] = (own + dot3(gating * attended, wo_v[...]))[:tok]

    @pl.when(p_row == r)
    def _():
        drain(rbuf.at[pl.ds(0, group - 1)], p_recv)

    @pl.when(p_row != r)
    def _():
        drain(rbuf, p_recv)

    half = cols // 2
    for q in range(cols):
        piece = rbuf[:, pl.ds(q, half, stride=cols), :]
        flip_v[:, q] = jnp.concatenate([piece[:, :, :bins], piece[:, :, bins:]], axis=1)
    logits = proj_v[...] + flip_v[...].reshape(total, bins) + bdist_v[...]
    expo = jnp.exp(logits - jnp.max(logits, axis=-1, keepdims=True))
    probs = expo / jnp.sum(expo, axis=-1, keepdims=True)
    theirs = jnp.broadcast_to(rbuf[:, packed:, :cols][:, None], (group, cols, cols, cols))
    fours = (group, cols, cols, cols)
    theirs = jnp.where(iota(fours, 3) == iota(fours, 1), theirs, 0.0).reshape(total, cols)
    theirs = mm(theirs.astype(BF16), ones)
    bin_id = iota((total, bins), 1).astype(F32)
    hot = (mine == bin_id).astype(F32) + (theirs == bin_id).astype(F32)
    pad_i = tokens[pl.ds(pl.multiple_of(r * rows, rows), rows), single_width:single_width + bins]
    pad_j = tokens[pl.ds(pl.multiple_of(c * cols, cols), cols), single_width:single_width + bins]
    mask = (pad_i[:, None, :] * pad_j[None, :, :]).reshape(total, bins)
    delta = mask * (2.0 * probs - hot)
    pair_o[...] = pair_o[...] + dot3(delta, dist_w)

    drain(gath.at[0, 0, pl.ds(0, n_row - 1)], g_send.at[0])
    drain(gath.at[pl.ds(0, chips - 1), 0], g_send.at[1])
    drain(gath.at[:, 0], g_send.at[2])
    drain(brecv.at[pl.ds(0, n_col - 1)], b_send)

    @pl.when(p_row == r)
    def _():
        drain(rbuf.at[pl.ds(0, group - 1)], p_send)

    @pl.when(p_row != r)
    def _():
        drain(rbuf, p_send)


def per_device(n_row, n_col, pair, single, target_bins, token_pad, *weights):
    rows, cols, width = pair.shape
    tok, single_width = single.shape
    w_gate, w_up, w_out, w_bias, w_query, w_key, w_value, w_gating, w_attn_out, w_dist, b_dist = weights
    heads = w_bias.shape[1]
    bins = w_dist.shape[1]
    w_bias, w_dist, target_bins = w_bias.T, w_dist.T, target_bins.T
    n_dev = n_row * n_col
    lanes = -(-tok * heads // 128) * 128
    group = rows // cols
    packed = cols * cols // 2
    b_dist = b_dist.reshape(1, bins)
    arrays = (pair, single, target_bins, token_pad, w_gate, w_up, w_out, w_bias, w_query, w_key, w_value, w_gating,
              w_attn_out, w_dist, b_dist)
    anywhere = pl.BlockSpec(memory_space=pl.ANY)
    vmem = pl.BlockSpec(memory_space=pltpu.VMEM)
    in_specs = [pl.BlockSpec(memory_space=pltpu.SMEM) if k == 3 else anywhere for k in range(len(arrays))]
    local = [pltpu.VMEM(a.shape, a.dtype) for k, a in enumerate(arrays) if k != 3]
    dma = pltpu.SemaphoreType.DMA
    pair_out, single_out = pl.pallas_call(
        functools.partial(kernel, n_row, n_col, heads),
        out_shape=(jax.ShapeDtypeStruct((rows * cols, width), F32), jax.ShapeDtypeStruct(single.shape, F32)),
        in_specs=in_specs,
        out_specs=(vmem, vmem),
        scratch_shapes=local + [
            pltpu.VMEM((tok, single_width + 128), F32),
            pltpu.VMEM((n_col // 2, 2, n_row, tok, single_width + 128), F32),
            pltpu.VMEM((n_dev * tok, single_width + 128), F32),
            pltpu.VMEM((rows * cols, width), F32),
            pltpu.VMEM((rows * cols, bins), F32),
            pltpu.VMEM((group, cols, cols, bins), F32),
            pltpu.VMEM((group, packed + cols, 128), F32),
            pltpu.VMEM((group, packed + cols, 128), F32),
            pltpu.VMEM((n_col, cols, lanes), F32),
            pltpu.VMEM((n_col, cols, lanes), F32),
            dma((len(arrays) - 1,)), dma((3,)), dma((3,)), dma, dma, dma, dma,
        ],
        compiler_params=pltpu.CompilerParams(
            collective_id=0, has_side_effects=True, vmem_limit_bytes=56 * 2**20
        ),
        name="pairformer_close",
    )(*arrays)
    return pair + pair_out.reshape(pair.shape), single_out


def solution(mesh):
    in_specs = (
        P("row", "col", None),
        P(("row", "col"), None),
        P("row", "col"),
        P(("row", "col")),
    ) + (P(),) * 11
    out_specs = (P("row", "col", None), P(("row", "col"), None))
    body = functools.partial(per_device, mesh.shape["row"], mesh.shape["col"])
    return jax.shard_map(body, mesh=mesh, in_specs=in_specs, out_specs=out_specs, check_vma=False)
```

```python
import functools

import jax
import jax.numpy as jnp
from jax import lax
from jax.experimental import pallas as pl
from jax.experimental.pallas import tpu as pltpu
from jax.sharding import PartitionSpec as P

MESH = pl.DeviceIdType.MESH
F32 = jnp.float32
BF16 = jnp.bfloat16
NN = (((1,), (0,)), ((), ()))
NT = (((1,), (1,)), ((), ()))
PARTS = 4


def split(x):
    high = x.astype(BF16)
    return high, (x - high.astype(F32)).astype(BF16)


def mm(a, b, dims=NN):
    return lax.dot_general(a, b, dims, preferred_element_type=F32)


def dot3(a, b, dims=NN):
    ah, al = split(a)
    bh, bl = b if isinstance(b, tuple) else split(b)
    rows = a.shape[0]
    if rows % 16:
        both = mm(jnp.concatenate([ah.astype(F32), al.astype(F32)], axis=0).astype(BF16), bh, dims)
    else:
        both = mm(jnp.concatenate([ah, al], axis=0), bh, dims)
    return both[:rows] + (both[rows:] + mm(ah, bl, dims))


def layer_norm(x):
    mean = jnp.mean(x, axis=-1, keepdims=True)
    centred = x - mean
    var = jnp.mean(centred * centred, axis=-1, keepdims=True)
    return centred * lax.rsqrt(var + 1e-05)


def iota(shape, axis):
    return lax.broadcasted_iota(jnp.int32, shape, axis)


def kernel(n_row, n_col, heads, *refs):
    (pair_h, single_h, target_h, pad_s, gate_h, up_h, wout_h, wbias_h, wq_h, wk_h, wv_h, wg_h, wo_h, wdist_h, bdist_h,
     pair_o, single_o,
     pair_v, single_v, target_v, gate_v, up_v, wout_v, wbias_v, wq_v, wk_v, wv_v, wg_v, wo_v, wdist_v, bdist_v,
     ext, gath, tokens, mid_v, proj_v, flip_v, sbuf, rbuf, tsend, trecv, bsend, brecv,
     in_sem, g_send, g_recv, b_send, b_recv, p_send, p_recv, t_send, t_recv) = refs
    rows, cols, width = pair_v.shape
    tok, single_width = single_v.shape
    bins = wdist_v.shape[0]
    group = rows // cols
    lanes = bsend.shape[2]
    head_dim = single_width // heads
    packed = cols * cols // 2
    r = lax.axis_index("row")
    c = lax.axis_index("col")

    sources = (single_h, pair_h, gate_h, up_h, wout_h, target_h, wbias_h, wdist_h, wk_h, wv_h, wq_h, wg_h, wo_h, bdist_h)
    targets = (single_v, pair_v, gate_v, up_v, wout_v, target_v, wbias_v, wdist_v, wk_v, wv_v, wq_v, wg_v, wo_v, bdist_v)
    loads = [pltpu.make_async_copy(a, b, in_sem.at[k]) for k, (a, b) in enumerate(zip(sources, targets))]
    for load in loads:
        load.start()

    chip, core = c // 2, lax.rem(c, 2)
    chips = n_col // 2
    p_row = c // group
    p_slot = lax.rem(c, group)
    at_home = p_row == r

    def is_self(k):
        return jnp.logical_and(at_home, p_slot == k)

    barrier = pltpu.get_barrier_semaphore()

    def greet(row, col):
        pl.semaphore_signal(barrier, inc=1, device_id=(row, col), device_id_type=MESH)

    for step in range(1, n_col):
        greet(r, lax.rem(c + step, n_col))
    for step in range(1, n_row):
        greet(lax.rem(r + step, n_row), c)

    @pl.when(jnp.logical_not(at_home))
    def _():
        for k in range(group):
            greet(p_row, group * r + k)

    loads[0].wait()
    row_id = iota((tok, 128), 0)
    pad_tile = jnp.zeros((tok, 128), F32)
    for q in range(tok):
        pad_tile = jnp.where(row_id == q, pad_s[q].astype(F32), pad_tile)
    ext[:, :single_width] = single_v[...]
    ext[:, single_width:] = pad_tile
    gath[chip, core, r] = ext[...]
    pl.semaphore_wait(barrier, n_col + n_row - 2 + jnp.where(at_home, 0, group))

    for step in range(1, n_row):
        pltpu.make_async_remote_copy(ext, gath.at[chip, core, r], g_send.at[0], g_recv.at[0], device_id=(lax.rem(r + step, n_row), c), device_id_type=MESH).start()

    for load in loads[1:8]:
        load.wait()

    gate_w = split(gate_v[...])
    up_w = split(up_v[...])
    out_w = split(wout_v[...])
    wdist = wdist_v[...]
    dist_w = split(wdist)
    none = jnp.zeros_like(wdist)
    wide = jnp.concatenate([jnp.concatenate([wdist, none], axis=1), jnp.concatenate([none, wdist], axis=1)], axis=0)
    wide_w = split(wide)
    slots = lanes // heads
    bias_rep = jnp.concatenate([wbias_v[...]] * slots, axis=0)
    row_q = iota((lanes, width), 0) // heads
    bias_w = split(jnp.concatenate([jnp.where(row_q == q, bias_rep, 0.0) for q in range(tok)], axis=1))

    bin_rows = target_v[...].astype(F32)
    eye = (iota((rows, rows), 0) == iota((rows, rows), 1)).astype(BF16)
    filled = jnp.concatenate([bin_rows, jnp.zeros((128 - cols, rows), F32)], axis=0).astype(BF16)
    tsend[...] = mm(eye, filled, NT).reshape(group, cols, 128)

    def send_bins(k, carry):
        @pl.when(jnp.logical_not(is_self(k)))
        def _():
            pltpu.make_async_remote_copy(tsend.at[k], trecv.at[p_slot], t_send, t_recv, device_id=(p_row, group * r + k), device_id_type=MESH).start()
        return carry

    lax.fori_loop(0, group, send_bins, 0)

    def drain(ref, sem):
        pltpu.make_async_copy(ref, ref, sem).wait()

    part = rows // PARTS

    def send_bias(d, carry):
        @pl.when(d != c)
        def _():
            pltpu.make_async_remote_copy(bsend.at[d], brecv.at[c], b_send, b_recv, device_id=(r, d), device_id_type=MESH).start()
        return carry

    def send_proj(k, carry):
        @pl.when(jnp.logical_not(is_self(k)))
        def _():
            pltpu.make_async_remote_copy(sbuf.at[k], rbuf.at[p_slot], p_send, p_recv, device_id=(p_row, group * r + k), device_id_type=MESH).start()
        return carry

    for s in range(PARTS):
        first = s * part
        x = pair_v[first:first + part].reshape(part * cols, width)
        normed = layer_norm(x)
        g = dot3(normed, gate_w)
        u = dot3(normed, up_w)
        hidden = g / (1.0 + jnp.exp(-g)) * u
        change = dot3(hidden, out_w)
        pair_o[first * cols:(first + part) * cols] = change
        mid = x + change
        mid_v[first * cols:(first + part) * cols] = mid
        tiles = part // cols
        halves = mid.reshape(tiles, 2, packed, width)
        both = jnp.concatenate([halves[:, 0].reshape(tiles * packed, width), halves[:, 1].reshape(tiles * packed, width)], axis=1)
        k0 = first // cols
        sbuf[k0:k0 + tiles] = dot3(both, wide_w, NT).reshape(tiles, packed, 2 * bins)
        lax.fori_loop(k0, k0 + tiles, send_proj, 0)
        dests = part // tok
        norm_mid = layer_norm(mid).reshape(dests, tok, cols, width)
        quad = jnp.concatenate([norm_mid[:, q].reshape(dests * cols, width) for q in range(tok)], axis=1)
        d0 = first // tok
        bsend[d0:d0 + dests] = dot3(quad, bias_w, NT).reshape(dests, cols, lanes)
        lax.fori_loop(d0, d0 + dests, send_bias, 0)
        if s == 0:
            drain(gath.at[0, 0, pl.ds(0, n_row - 1)], g_recv.at[0])
            for step in range(1, chips):
                pltpu.make_async_remote_copy(gath.at[chip, core], gath.at[chip, core], g_send.at[1], g_recv.at[1], device_id=(r, lax.rem(c + 2 * step, n_col)), device_id_type=MESH).start()
        if s == PARTS // 2:
            drain(gath.at[pl.ds(0, chips - 1), 0], g_recv.at[1])
            pltpu.make_async_remote_copy(gath.at[:, core], gath.at[:, core], g_send.at[2], g_recv.at[2], device_id=(r, c + 1 - 2 * core), device_id_type=MESH).start()

    brecv[c] = bsend[c]

    @pl.when(p_row == r)
    def _():
        rbuf[p_slot] = sbuf[p_slot]
        trecv[p_slot] = tsend[p_slot]

    for load in loads[8:]:
        load.wait()

    own = jnp.concatenate([single_v[...], jnp.zeros((slots - tok, single_width), F32)], axis=0)
    own_norm = layer_norm(own)
    query = dot3(own_norm, wq_v[...])
    gating = jax.nn.sigmoid(dot3(own_norm, wg_v[...]))
    total = rows * cols
    proj_v[...] = dot3(mid_v[...], dist_w, NT)
    ones = jnp.ones((cols, bins), BF16)
    three = (rows, cols, rows)
    mine = jnp.where(iota(three, 2) == iota(three, 0), jnp.broadcast_to(bin_rows[None], three), 0.0).reshape(total, rows)
    mine = mm(mine.astype(BF16), jnp.ones((rows, bins), BF16))
    drain(gath.at[:, 0], g_recv.at[2])
    step = 8 // tok
    for row in range(n_row):
        for m in range(0, n_col, step):
            at = (row * n_col + m) * tok
            tokens[at:at + 8, :] = jnp.concatenate([gath[(m + q) // 2, (m + q) % 2, row] for q in range(step)], axis=0)
    everyone = layer_norm(tokens[:, :single_width])
    key = dot3(everyone, wk_v[...])
    value = dot3(everyone, wv_v[...])
    head_mask = (iota((heads, single_width), 1) // head_dim == iota((heads, single_width), 0)).astype(F32)
    query_wide = (query[:, None, :] * head_mask[None]).reshape(lanes, single_width)
    scores = dot3(key, query_wide, NT) * (1.0 / head_dim ** 0.5)
    pads = tokens[:, single_width:]

    drain(brecv.at[pl.ds(0, n_col - 1)], b_recv)
    scores = scores + brecv[...].reshape(scores.shape)
    scores = jnp.where(pads > 0.5, scores, -1e9)
    expo = jnp.exp(scores - jnp.max(scores, axis=0, keepdims=True))
    weights = expo / jnp.sum(expo, axis=0, keepdims=True)
    mixed = dot3(jnp.transpose(weights), value).reshape(slots, heads, single_width)
    attended = jnp.sum(mixed * head_mask[None], axis=1)
    single_o[...] = (own + dot3(gating * attended, wo_v[...]))[:tok]

    @pl.when(p_row == r)
    def _():
        drain(trecv.at[pl.ds(0, group - 1)], t_recv)
        drain(rbuf.at[pl.ds(0, group - 1)], p_recv)

    @pl.when(p_row != r)
    def _():
        drain(trecv, t_recv)
        drain(rbuf, p_recv)

    half = cols // 2
    for q in range(cols):
        piece = rbuf[:, pl.ds(q, half, stride=cols), :]
        flip_v[:, q] = jnp.concatenate([piece[:, :, :bins], piece[:, :, bins:]], axis=1)
    logits = proj_v[...] + flip_v[...].reshape(total, bins) + bdist_v[...]
    expo = jnp.exp(logits - jnp.max(logits, axis=-1, keepdims=True))
    probs = expo / jnp.sum(expo, axis=-1, keepdims=True)
    theirs = jnp.broadcast_to(trecv[:, :, :cols][:, None], (group, cols, cols, cols))
    fours = (group, cols, cols, cols)
    theirs = jnp.where(iota(fours, 3) == iota(fours, 1), theirs, 0.0).reshape(total, cols)
    theirs = mm(theirs.astype(BF16), ones)
    bin_id = iota((total, bins), 1).astype(F32)
    hot = (mine == bin_id).astype(F32) + (theirs == bin_id).astype(F32)
    pad_i = tokens[pl.ds(pl.multiple_of(r * rows, rows), rows), single_width:single_width + bins]
    pad_j = tokens[pl.ds(pl.multiple_of(c * cols, cols), cols), single_width:single_width + bins]
    mask = (pad_i[:, None, :] * pad_j[None, :, :]).reshape(total, bins)
    delta = mask * (2.0 * probs - hot)
    pair_o[...] = pair_o[...] + dot3(delta, dist_w)

    drain(gath.at[0, 0, pl.ds(0, n_row - 1)], g_send.at[0])
    drain(gath.at[pl.ds(0, chips - 1), 0], g_send.at[1])
    drain(gath.at[:, 0], g_send.at[2])
    drain(brecv.at[pl.ds(0, n_col - 1)], b_send)

    @pl.when(p_row == r)
    def _():
        drain(trecv.at[pl.ds(0, group - 1)], t_send)
        drain(rbuf.at[pl.ds(0, group - 1)], p_send)

    @pl.when(p_row != r)
    def _():
        drain(trecv, t_send)
        drain(rbuf, p_send)


def per_device(n_row, n_col, pair, single, target_bins, token_pad, *weights):
    rows, cols, width = pair.shape
    tok, single_width = single.shape
    w_gate, w_up, w_out, w_bias, w_query, w_key, w_value, w_gating, w_attn_out, w_dist, b_dist = weights
    heads = w_bias.shape[1]
    bins = w_dist.shape[1]
    w_bias, w_dist, target_bins = w_bias.T, w_dist.T, target_bins.T
    n_dev = n_row * n_col
    lanes = -(-tok * heads // 128) * 128
    group = rows // cols
    packed = cols * cols // 2
    b_dist = b_dist.reshape(1, bins)
    arrays = (pair, single, target_bins, token_pad, w_gate, w_up, w_out, w_bias, w_query, w_key, w_value, w_gating,
              w_attn_out, w_dist, b_dist)
    anywhere = pl.BlockSpec(memory_space=pl.ANY)
    vmem = pl.BlockSpec(memory_space=pltpu.VMEM)
    in_specs = [pl.BlockSpec(memory_space=pltpu.SMEM) if k == 3 else anywhere for k in range(len(arrays))]
    local = [pltpu.VMEM(a.shape, a.dtype) for k, a in enumerate(arrays) if k != 3]
    dma = pltpu.SemaphoreType.DMA
    pair_out, single_out = pl.pallas_call(
        functools.partial(kernel, n_row, n_col, heads),
        out_shape=(jax.ShapeDtypeStruct((rows * cols, width), F32), jax.ShapeDtypeStruct(single.shape, F32)),
        in_specs=in_specs,
        out_specs=(vmem, vmem),
        scratch_shapes=local + [
            pltpu.VMEM((tok, single_width + 128), F32),
            pltpu.VMEM((n_col // 2, 2, n_row, tok, single_width + 128), F32),
            pltpu.VMEM((n_dev * tok, single_width + 128), F32),
            pltpu.VMEM((rows * cols, width), F32),
            pltpu.VMEM((rows * cols, bins), F32),
            pltpu.VMEM((group, cols, cols, bins), F32),
            pltpu.VMEM((group, packed, 128), F32),
            pltpu.VMEM((group, packed, 128), F32),
            pltpu.VMEM((group, cols, 128), F32),
            pltpu.VMEM((group, cols, 128), F32),
            pltpu.VMEM((n_col, cols, lanes), F32),
            pltpu.VMEM((n_col, cols, lanes), F32),
            dma((len(arrays) - 1,)), dma((3,)), dma((3,)), dma, dma, dma, dma, dma, dma,
        ],
        compiler_params=pltpu.CompilerParams(
            collective_id=0, has_side_effects=True, vmem_limit_bytes=56 * 2**20
        ),
        name="pairformer_close",
    )(*arrays)
    return pair + pair_out.reshape(pair.shape), single_out


def solution(mesh):
    in_specs = (
        P("row", "col", None),
        P(("row", "col"), None),
        P("row", "col"),
        P(("row", "col")),
    ) + (P(),) * 11
    out_specs = (P("row", "col", None), P(("row", "col"), None))
    body = functools.partial(per_device, mesh.shape["row"], mesh.shape["col"])
    return jax.shard_map(body, mesh=mesh, in_specs=in_specs, out_specs=out_specs, check_vma=False)
```
